32 devices in a mesh: ctx: 8 (over z, x), tp: 4 (over y, core).
Axes of the slice: x: 2, y: 2, z: 4, core: 2. Of those that a mesh axis runs over, the one named last changes fastest.
Arguments:
- hidden: bfloat16 [2048, 2048], P(('ctx', 'tp')), may hold values from -14 to 14
- in_weight: bfloat16 [2048, 2, 4096], P(None, None, 'tp'), may hold values from -0.125 to 0.125
- step_weight: bfloat16 [2048, 64], P(None, 'tp'), may hold values from -0.125 to 0.125
- group_weight: bfloat16 [256, 4, 2048], P('tp'), may hold values from -0.125 to 0.125
- conv_inner: float32 [4, 4096], P(None, 'tp'), may hold values from -3 to 3
- inner_bias: float32 [4096], P('tp'), may hold values from -2.5 to 2.5
- conv_group: float32 [4, 1024], replicated, may hold values from -3 to 3
- group_bias: float32 [1024], replicated, may hold values from -2.5 to 2.5
- step_bias: float32 [64], P('tp'), may hold values from -9.5 to 0
- log_rate: float32 [64], P('tp'), may hold values from -2.5 to -0.5
- skip_weight: float32 [64], P('tp'), may hold values from 0.25 to 1
- norm_gain: float32 [4096], P('tp'), may hold values from 0.1 to 1.9
- out_weight: bfloat16 [4096, 2048], P('tp'), may hold values from -0.09375 to 0.09375
Outputs:
- mixed: bfloat16 [2048, 2048], P(('ctx', 'tp'))
The draws below stay inside these ranges and needn't reach their ends.
All inputs are finite; a program needn't handle non-finite values.
Results may differ from the reference program's by a relative error of at most 0.024.
Values may be sent and summed in bfloat16 or wider, within the bound.
A program may use at most 64 MiB of HBM per device.

```python
import jax
import jax.numpy as jnp
from jax import lax

D = 2048
HEADS = 64
HEAD_DIM = 64
STATE = 128
GROUPS = 4
BLOCK = 256
KERNEL = 4
SEQUENCE_LENGTH = 2048
INNER = 4096


def draw_hidden(key, part):
    root_random_key = jax.random.fold_in(key, 0)
    segment_random_key = jax.random.fold_in(key, 2)
    value_entries = jax.random.truncated_normal(root_random_key, -2.0, 2.0, (SEQUENCE_LENGTH, D), jnp.float32)
    segment_runs = jax.random.uniform(segment_random_key, (SEQUENCE_LENGTH, 1), jnp.float32) < 1.0 / 1024
    return jnp.where(segment_runs, 4.0 * value_entries, value_entries).astype(jnp.bfloat16)


def draw_step_bias(key, part):
    pick_key, slow_key, fast_key = jax.random.split(key, 3)
    fraction = 0.5
    chooser = jax.random.uniform(pick_key, (HEADS,), jnp.float32)
    slow_value = jax.random.uniform(slow_key, (HEADS,), jnp.float32, -9.5, -8.5)
    fast_value = jax.random.uniform(fast_key, (HEADS,), jnp.float32, -2.0, 0.0)
    return jnp.where(chooser < fraction, slow_value, fast_value)


def steps_of(key, dims, pieces, smallest, top_value):
    def one(dim, parts):
        draws = jax.random.uniform(jax.random.fold_in(jax.random.fold_in(key, 6), dim), (parts,), jnp.float32, smallest / len(pieces), top_value / len(pieces))
        return jnp.repeat(jnp.exp(draws), dims[dim] // parts).reshape((-1,) + (1,) * (len(dims) - dim - 1))

    gain = one(*pieces[0])
    for cut in pieces[1:]:
        gain = gain * one(*cut)
    return gain


def centred(own_key, dims, width, reach, shards=(), held_as=jnp.bfloat16):
    entries = jax.random.normal(own_key, dims, jnp.float32) * width
    if len(shards) > 0:
        entries = steps_of(own_key, dims, shards, -0.22, 0.18) * entries
    return jnp.clip(entries, min=-reach, max=reach).astype(held_as)


def setup_inputs(seed: int = 0) -> dict:
    arg_keys = jax.random.split(jax.random.key(seed), 14)
    return {
        "hidden": draw_hidden(jax.random.fold_in(arg_keys[13], 71), 0),
        "in_weight": centred(arg_keys[1], (D, 2, INNER), D ** -0.5, 0.125, ((2, 4),)),
        "step_weight": centred(arg_keys[2], (D, HEADS), D ** -0.5, 0.125, ((1, 4),)),
        "group_weight": centred(arg_keys[3], (2 * STATE, GROUPS, D), D ** -0.5, 0.125, ((0, 4),)),
        "conv_inner": centred(arg_keys[4], (KERNEL, INNER), KERNEL ** -0.5, 3.0, ((1, 4),), jnp.float32),
        "inner_bias": centred(arg_keys[5], (INNER,), 0.5, 2.5, ((0, 4),), jnp.float32),
        "conv_group": centred(arg_keys[6], (KERNEL, 2 * GROUPS * STATE), KERNEL ** -0.5, 3.0, (), jnp.float32),
        "group_bias": centred(arg_keys[7], (2 * GROUPS * STATE,), 0.5, 2.5, (), jnp.float32),
        "step_bias": draw_step_bias(jax.random.fold_in(arg_keys[13], 71), 0),
        "log_rate": jnp.clip(-2.5 + 2.0 * jax.random.uniform(arg_keys[9], (HEADS,), jnp.float32) ** steps_of(arg_keys[9], (HEADS,), ((0, 4),), -0.2, 0.2), -2.5, -0.5),
        "skip_weight": jnp.clip(0.25 + 0.75 * jax.random.uniform(arg_keys[10], (HEADS,), jnp.float32) ** steps_of(arg_keys[10], (HEADS,), ((0, 4),), -0.2, 0.2), 0.25, 1.0),
        "norm_gain": jnp.clip(1.0 + 0.18 * jax.random.normal(arg_keys[11], (INNER,), jnp.float32), 0.1, 1.9),
        "out_weight": centred(arg_keys[12], (INNER, D), INNER ** -0.5, 0.09375, ((0, 4),)),
    }


def causal_conv(prior_rows, raw_rows, conv_weight, conv_bias):
    joined = jnp.concatenate([prior_rows, raw_rows], axis=0).astype(jnp.float32)
    length = raw_rows.shape[0]
    running = jnp.broadcast_to(conv_bias.astype(jnp.float32)[None, :], raw_rows.shape)
    for offset in range(conv_weight.shape[0]):
        running = running + conv_weight[offset][None, :] * joined[offset:offset + length]
    return jax.nn.silu(running).astype(jnp.bfloat16)

def reference(hidden, in_weight, step_weight, group_weight, conv_inner, inner_bias, conv_group, group_bias, step_bias, log_rate, skip_weight, norm_gain, out_weight):
    highest = lax.Precision.HIGHEST
    zx_rows = jnp.dot(hidden, in_weight.reshape(D, 2 * INNER), preferred_element_type=jnp.float32).astype(jnp.bfloat16)
    gate_raw = zx_rows[:, :INNER]
    inner_raw = zx_rows[:, INNER:]
    group_matrix = jnp.transpose(group_weight, (1, 0, 2)).reshape(GROUPS * 2 * STATE, D)
    map_raw = lax.dot_general(hidden, group_matrix, (((1,), (1,)), ((), ())), preferred_element_type=jnp.float32).astype(jnp.bfloat16)
    step_raw = jnp.dot(hidden, step_weight, preferred_element_type=jnp.float32).astype(jnp.bfloat16)
    x_conv = causal_conv(jnp.zeros((KERNEL - 1, INNER), jnp.bfloat16), inner_raw, conv_inner, inner_bias)
    maps = causal_conv(jnp.zeros((KERNEL - 1, 2 * GROUPS * STATE), jnp.bfloat16), map_raw, conv_group, group_bias)
    maps = maps.reshape(SEQUENCE_LENGTH, GROUPS, 2, STATE)
    step_size = jax.nn.softplus(step_raw.astype(jnp.float32) + step_bias[None, :])
    decay_rate = -jnp.exp(log_rate)
    blocks = SEQUENCE_LENGTH // BLOCK
    per_group = HEADS // GROUPS
    x_blocks = x_conv.reshape(blocks, BLOCK, HEADS, HEAD_DIM)
    input_map = maps[:, :, 0, :].reshape(blocks, BLOCK, GROUPS, STATE)
    output_map = maps[:, :, 1, :].reshape(blocks, BLOCK, GROUPS, STATE)
    step_blocks = step_size.reshape(blocks, BLOCK, HEADS)
    causal = jnp.arange(BLOCK)[:, None] >= jnp.arange(BLOCK)[None, :]

    def block_step(carry, item):
        x_vals, in_map, out_map, steps_here = item
        log_step = (steps_here * decay_rate[None, :]).T
        cumulative = jnp.cumsum(log_step, axis=1)
        scores = jnp.einsum('ign,jgn->gij', out_map.astype(jnp.float32), in_map.astype(jnp.float32), precision=highest)
        scores = jnp.repeat(scores, per_group, axis=0)
        exponent = jnp.where(causal[None], cumulative[:, :, None] - cumulative[:, None, :], -jnp.inf)
        mixing = (scores * jnp.exp(exponent) * steps_here.T[:, None, :]).astype(jnp.bfloat16)
        mixing = lax.optimization_barrier(mixing).astype(jnp.float32)
        x_float = x_vals.astype(jnp.float32)
        within = jnp.einsum('hij,jhp->ihp', mixing, x_float, precision=highest)
        out_heads = jnp.repeat(out_map, per_group, axis=1).astype(jnp.float32)
        in_heads = jnp.repeat(in_map, per_group, axis=1).astype(jnp.float32)
        start_low = lax.optimization_barrier(carry.astype(jnp.bfloat16)).astype(jnp.float32)
        carried = jnp.exp(cumulative).T[:, :, None] * jnp.einsum('ihn,hpn->ihp', out_heads, start_low, precision=highest)
        weight = jnp.exp(cumulative[:, -1:] - cumulative) * steps_here.T
        weighted = (x_float * weight.T[:, :, None]).astype(jnp.bfloat16)
        weighted = lax.optimization_barrier(weighted).astype(jnp.float32)
        block_state = jnp.einsum('jhp,jhn->hpn', weighted, in_heads, precision=highest)
        result_heads = within + carried + skip_weight[None, :, None] * x_float
        following = jnp.exp(cumulative[:, -1])[:, None, None] * carry + block_state
        return (following, result_heads)
    initial = jnp.zeros((HEADS, HEAD_DIM, STATE), jnp.float32)
    final_state, result_blocks = lax.scan(block_step, initial, (x_blocks, input_map, output_map, step_blocks))
    result_heads = result_blocks.reshape(SEQUENCE_LENGTH, INNER)
    gated = result_heads * jax.nn.silu(gate_raw.astype(jnp.float32))
    grouped = gated.reshape(SEQUENCE_LENGTH, GROUPS, INNER // GROUPS)
    inverse = lax.rsqrt(lax.optimization_barrier(jnp.mean(grouped * grouped, axis=2)) + 1e-05)
    normed = ((grouped * inverse[:, :, None]).reshape(SEQUENCE_LENGTH, INNER) * norm_gain[None, :]).astype(jnp.bfloat16)
    return jnp.dot(normed, out_weight, preferred_element_type=jnp.float32).astype(jnp.bfloat16)
```

```python
import functools

import jax
import jax.numpy as jnp
from jax import lax
from jax.experimental import pallas as pl
from jax.experimental.pallas import tpu as pltpu
from jax.sharding import PartitionSpec as P

HEADS = 64
HEAD_DIM = 64
STATE = 128
GROUPS = 4
KERNEL = 4
PAD = 16
LANES = 128
F32 = jnp.float32
BF16 = jnp.bfloat16
NT = (((1,), (1,)), ((), ()))


def dot(a, b):
    return jnp.dot(a, b, preferred_element_type=F32)


def dot_nt(a, b):
    return lax.dot_general(a, b, NT, preferred_element_type=F32)


def silu(v):
    half = 0.5 * v
    return half + half * jnp.tanh(half)


def softplus(v):
    e = jnp.exp(-jnp.abs(v))
    small = e * (1.0 - e * (0.5 - e * (1.0 / 3.0)))
    return jnp.maximum(v, 0.0) + jnp.where(e < 0.01, small, jnp.log(1.0 + e))


def split_terms(a):
    hi = a.astype(BF16)
    lo = (a - hi.astype(F32)).astype(BF16)
    return jnp.concatenate([hi, lo], axis=1)


def iota(shape, dim):
    return lax.broadcasted_iota(jnp.int32, shape, dim)


def kernel(
    sizes,
    hidden, in_w, step_w, group_w, conv_inner, inner_bias, conv_group, group_bias,
    step_bias, log_rate, skip_weight, norm_gain, out_w,
    out,
    xbuf, w_vm, gw_vm, ow_vm, sw_pad, rows_pad, xeo, raw, gate_buf, map_send, map_recv,
    map_raw, x_buf, st_send, st_recv, dec_buf, dec_recv, start_out, start_buf, xt_buf, gated_buf, nbuf,
    rs_send1, rs_recv1, s_buf, rs_send2, rs_recv2, sq_send, sq_recv,
    w_sem, gw_sem, ow_sem, own_sem,
    ys_sem, yr_sem, ps_sem, pr_sem, hs_sem, hr_sem,
    ms_sem, mr_sem, ss_sem, sr_sem, ds_sem, dr_sem, bs_sem, br_sem,
    q1s_sem, q1r_sem, q2s_sem, q2r_sem, sqs_sem, sqr_sem,
):
    C, T = sizes
    Y = T // 2
    r = hidden.shape[0]
    R = r * T
    D = hidden.shape[1]
    inner = out_w.shape[0]
    heads = step_w.shape[0]
    m_dev = group_w.shape[0]
    span = T // GROUPS
    NS = st_send.shape[0]
    slice_rows = STATE // NS
    stride = C // NS
    NC = rs_send1.shape[0]
    cols = rs_send1.shape[2]
    c = lax.axis_index("ctx")
    t = lax.axis_index("tp")
    y = t // 2
    core = t % 2
    group = t // span

    def at(cc, tt):
        return {"ctx": cc, "tp": tt}

    def remote(src, dst, ssem, rsem, cc, tt):
        return pltpu.make_async_remote_copy(
            src_ref=src, dst_ref=dst, send_sem=ssem, recv_sem=rsem,
            device_id=(cc, tt), device_id_type=pl.DeviceIdType.MESH,
        )

    gws = [
        pltpu.make_async_copy(group_w.at[:, :, pl.ds(k * LANES, LANES)], gw_vm.at[k], gw_sem.at[k])
        for k in range(D // LANES)
    ]
    ws = [
        pltpu.make_async_copy(in_w.at[:, :, pl.ds(k * LANES, LANES)], w_vm.at[k], w_sem.at[k])
        for k in range(inner // LANES)
    ]
    ow = pltpu.make_async_copy(out_w, ow_vm, ow_sem)
    own = pltpu.make_async_copy(hidden, xbuf.at[pl.ds(PAD + t * r, r)], own_sem)
    own.start()
    for cp in gws:
        cp.start()
    for cp in ws:
        cp.start()
    ow.start()

    barrier = pltpu.get_barrier_semaphore()

    def greet(cc, tt):
        pl.semaphore_signal(barrier, inc=1, device_id=(cc, tt), device_id_type=pl.DeviceIdType.MESH)

    for d in range(1, T):
        greet(c, (t + d) % T)
    for d in range(1, C):
        greet((c + d) % C, t)
    has_next = jnp.logical_and(t == T - 1, c < C - 1)

    @pl.when(c > 0)
    def _():
        greet(c - 1, T - 1)

    pl.semaphore_wait(barrier, T - 1 + C - 1 + jnp.where(has_next, T, 0))

    row_of = lambda s: pl.ds(PAD + s * r, r)
    partner = y * 2 + (1 - core)
    y_copies = []
    for d in range(1, Y):
        tt = ((y + d) % Y) * 2 + core
        cp = remote(hidden, xbuf.at[row_of(t)], ys_sem.at[d], yr_sem.at[d], c, tt)
        cp.start()
        y_copies.append(cp)
    first = remote(hidden, xbuf.at[row_of(t)], ps_sem.at[0], pr_sem.at[0], c, partner)
    first.start()

    @pl.when(has_next)
    def _():
        for tt in range(T):
            remote(hidden.at[pl.ds(r - PAD, PAD)], xbuf.at[pl.ds(0, PAD)],
                   hs_sem.at[tt], hr_sem, c + 1, tt).start()

    @pl.when(c == 0)
    def _():
        xbuf[pl.ds(0, PAD), :] = jnp.zeros((PAD, D), BF16)

    sw_pad[...] = jnp.zeros(sw_pad.shape, BF16)
    sw_pad[pl.ds(0, heads), :] = step_w[...]
    rows_pad[...] = jnp.zeros(rows_pad.shape, F32)
    rows_pad[pl.ds(0, 1), pl.ds(0, heads)] = step_bias[...]
    rows_pad[pl.ds(1, 1), pl.ds(0, heads)] = log_rate[...]
    rows_pad[pl.ds(2, 1), pl.ds(0, heads)] = skip_weight[...]

    forwards = []
    for d in range(1, Y):
        src = ((y + Y - d) % Y) * 2 + core
        y_copies[d - 1].wait_recv()
        cp = remote(xbuf.at[row_of(src)], xbuf.at[row_of(src)], ps_sem.at[d], pr_sem.at[d], c, partner)
        cp.start()
        forwards.append(cp)
    own.wait()
    first.wait_recv()
    for cp in forwards:
        cp.wait_recv()

    @pl.when(c > 0)
    def _():
        remote(hidden.at[pl.ds(r - PAD, PAD)], xbuf.at[pl.ds(0, PAD)],
               hs_sem.at[0], hr_sem, c, t).wait_recv()

    for cp in gws:
        cp.wait()
    gw = jnp.concatenate(
        [gw_vm[k].reshape(m_dev * GROUPS, LANES) for k in range(D // LANES)], axis=1
    )
    mt = dot_nt(gw, xbuf[...]).astype(BF16)
    q = m_dev * GROUPS
    dst_row, src_row = iota((q, q), 0), iota((q, q), 1)
    order = (src_row == (dst_row % m_dev) * GROUPS + dst_row // m_dev).astype(F32).astype(BF16)
    mt = dot(order, mt).astype(BF16)
    map_send[...] = mt.reshape(map_send.shape)
    m_copies = []
    for d in range(1, T):
        tt = (t + d) % T
        cp = remote(map_send.at[tt // span], map_recv.at[t], ms_sem.at[d], mr_sem.at[d], c, tt)
        cp.start()
        m_copies.append(cp)
    map_recv[t] = map_send[group]

    step_raw = dot_nt(xbuf[pl.ds(PAD, R), :], sw_pad[...]).astype(BF16).astype(F32)
    step = softplus(step_raw + rows_pad[0:1, :])
    log_step = -jnp.exp(rows_pad[1:2, :]) * step
    lower = (iota((R, R), 0) >= iota((R, R), 1)).astype(F32)
    cum = lax.dot_general(
        lower, log_step, (((1,), (0,)), ((), ())),
        preferred_element_type=F32, precision=lax.Precision.HIGHEST,
    )
    cum_t = cum.T
    last = cum[R - 1 : R, :]
    own_decay = jnp.exp(jnp.broadcast_to(last, (8, LANES)))
    dec_buf[...] = own_decay
    d_copies = []
    for d in range(1, C):
        cc = (c + d) % C
        cp = remote(dec_buf, dec_recv.at[c], ds_sem.at[d], dr_sem.at[d], cc, t)
        cp.start()
        d_copies.append(cp)
    dec_recv[c] = own_decay
    spread_row = iota((2 * LANES, inner), 0) % LANES
    spread = (spread_row == iota((2 * LANES, inner), 1) // HEAD_DIM).astype(F32).astype(BF16)
    step_wide = dot(split_terms(step), spread)
    tail_wide = dot(split_terms(jnp.exp(jnp.minimum(last - cum, 0.0)) * step), spread)
    cum_wide = dot(split_terms(jnp.exp(cum)), spread)
    skip_wide = dot(split_terms(rows_pad[...]), spread)[2:3, :]

    sel_r, sel_c = iota((LANES, 2 * LANES), 0), iota((LANES, 2 * LANES), 1)
    even = (sel_c == 2 * sel_r).astype(F32).astype(BF16)
    odd = (sel_c == 2 * sel_r + 1).astype(F32).astype(BF16)
    M = R + PAD
    for k in range(D // LANES):
        piece = xbuf[:, pl.ds(k * LANES, LANES)]
        xeo[pl.ds(0, R), pl.ds(2 * k * LANES, 2 * LANES)] = dot(piece[PAD:], even).astype(BF16)
        xeo[pl.ds(R, M), pl.ds(2 * k * LANES, 2 * LANES)] = dot(piece, odd).astype(BF16)
    for n in range(inner // (2 * LANES)):
        ws[2 * n].wait()
        ws[2 * n + 1].wait()
        w = jnp.concatenate(
            [w_vm[2 * n].reshape(2 * D, LANES), w_vm[2 * n + 1].reshape(2 * D, LANES)], axis=1
        )
        z = dot(xeo[...], w).astype(BF16)
        sl = pl.ds(2 * n * LANES, 2 * LANES)
        gate_buf[:, sl] = z[:R]
        raw[...] = z[R:].astype(F32)
        acc = inner_bias[:, sl]
        for k in range(KERNEL):
            acc = acc + conv_inner[k : k + 1, sl] * raw[pl.ds(PAD - KERNEL + 1 + k, R), :]
        x_buf[:, sl] = silu(acc).astype(BF16)

    for cp in m_copies:
        cp.wait_recv()
    eye = (iota((M, M), 0) == iota((M, M), 1)).astype(F32).astype(BF16)
    map_raw[...] = dot_nt(eye, map_recv[...].reshape(2 * STATE, M))
    gsl = pl.ds(pl.multiple_of(group * 2 * STATE, 2 * STATE), 2 * STATE)
    acc = group_bias[:, gsl]
    for k in range(KERNEL):
        acc = acc + conv_group[k : k + 1, gsl] * map_raw[pl.ds(PAD - KERNEL + 1 + k, R), :]
    maps = silu(acc).astype(BF16)
    b_map = maps[:, :STATE]
    c_map = maps[:, STATE:]
    eye_b = (iota((STATE, STATE), 0) == iota((STATE, STATE), 1)).astype(F32).astype(BF16)
    b_t = dot_nt(eye_b, b_map).astype(BF16)

    x_float = x_buf[...].astype(F32)
    weighted = (x_float * tail_wide).astype(BF16)
    state = dot(b_t, weighted)
    st_send[...] = state.astype(BF16).reshape(st_send.shape)
    for d in range(1, C):
        cc = (c + d) % C

        def send_state(cc=cc, d=d):
            remote(st_send.at[cc // stride], st_recv.at[c], ss_sem.at[d], sr_sem.at[d], cc, t).start()

        if stride == 1:
            send_state()
        else:
            pl.when(cc % stride == 0)(send_state)
    mine = c // stride
    st_recv[c] = st_send[mine]
    xt_buf[...] = (x_float * step_wide).astype(BF16)

    def mixing(pairs):
        scores = dot_nt(c_map, b_map) * lower
        half = R // 2
        for p in pairs:
            sl = pl.ds(p * LANES, LANES)
            xt = xt_buf[:, sl]
            parts = []
            for h in (2 * p, 2 * p + 1):
                col = cum[:, h : h + 1]
                row = cum_t[h : h + 1, :]
                top = jnp.exp(jnp.minimum(col[:half] - row[:, :half], 0.0)) * scores[:half, :half]
                bot = jnp.exp(jnp.minimum(col[half:] - row, 0.0)) * scores[half:]
                parts.append(
                    jnp.concatenate(
                        [dot(top.astype(BF16), xt[:half]), dot(bot.astype(BF16), xt)], axis=0
                    )
                )
            lane = iota((R, LANES), 1)
            gated_buf[:, sl] = jnp.where(lane < HEAD_DIM, parts[0], parts[1])

    pairs = inner // LANES
    cut = pairs // 2
    mixing(range(cut))

    def prefix():
        for d in range(1, C):
            remote(st_send.at[0], st_recv.at[c], ss_sem.at[d], sr_sem.at[d], c, t).wait_recv()
        running = jnp.zeros((slice_rows, inner), F32)
        for k in range(C):
            start_out[k] = running.astype(BF16)
            decay = dot(split_terms(dec_recv[k]), spread)[0:1, :]
            running = running * decay + st_recv[k].astype(F32)
        for d in range(1, C):
            cc = (c + d) % C
            remote(start_out.at[cc], start_buf.at[mine], bs_sem.at[d], br_sem.at[d], cc, t).start()
        start_buf[mine] = start_out[c]

    for cp in d_copies:
        cp.wait_recv()
    if stride == 1:
        prefix()
    else:
        pl.when(c % stride == 0)(prefix)

    mixing(range(cut, pairs))

    for d in range(1, C):
        def wait_start(d=d):
            remote(start_out.at[0], start_buf.at[mine], bs_sem.at[d], br_sem.at[d], c, t).wait_recv()

        if stride == 1:
            wait_start()
        else:
            pl.when((c + C - d) % C % stride == 0)(wait_start)
    starts = start_buf[...].reshape(STATE, inner)
    squares = jnp.zeros((R, LANES), F32)
    for p in range(pairs):
        sl = slice(p * LANES, (p + 1) * LANES)
        carried = dot(c_map, starts[:, sl]) * cum_wide[:, sl]
        value = gated_buf[:, sl] + carried + skip_wide[:, sl] * x_buf[:, sl].astype(F32)
        value = value * silu(gate_buf[:, sl].astype(F32))
        gated_buf[:, sl] = value
        squares = squares + value * value
    total = jnp.sum(squares, axis=1, keepdims=True)
    if span > 1:
        sq_send[...] = jnp.broadcast_to(total, (R, LANES))
        sq_copies = []
        for d in range(1, span):
            tt = group * span + (t % span + d) % span
            cp = remote(sq_send, sq_recv.at[d], sqs_sem.at[d], sqr_sem.at[d], c, tt)
            cp.start()
            sq_copies.append(cp)
        for d in range(1, span):
            sq_copies[d - 1].wait_recv()
            total = total + sq_recv[d][:, 0:1]
    inverse = lax.rsqrt(total / (HEADS * HEAD_DIM // GROUPS) + 1e-05)
    normed = (gated_buf[...] * inverse * norm_gain[...]).astype(BF16)
    nbuf[...] = normed.reshape(T, r, inner)

    ow.wait()
    other = jnp.concatenate([nbuf[2 * j + (1 - core)] for j in range(Y)], axis=0)
    q1 = []
    for n in range(NC):
        rs_send1[n] = dot(other, ow_vm[:, pl.ds(n * cols, cols)]).astype(BF16)
        cp = remote(rs_send1.at[n], rs_recv1.at[n], q1s_sem.at[n], q1r_sem.at[n], c, partner)
        cp.start()
        q1.append(cp)
    same = jnp.concatenate([nbuf[2 * j + core] for j in range(Y)], axis=0)
    q2 = []
    for n in range(NC):
        part = dot(same, ow_vm[:, pl.ds(n * cols, cols)])
        q1[n].wait_recv()
        s_buf[n] = (part + rs_recv1[n].astype(F32)).reshape(Y, r, cols)
        for d in range(1, Y):
            yy = (y + d) % Y
            rs_send2[n, d] = s_buf[n, yy].astype(BF16)
            cp = remote(rs_send2.at[n, d], rs_recv2.at[n, d], q2s_sem.at[n, d], q2r_sem.at[n, d],
                        c, yy * 2 + core)
            cp.start()
            q2.append(cp)
    for n in range(NC):
        part = s_buf[n, y]
        for d in range(1, Y):
            q2[n * (Y - 1) + d - 1].wait_recv()
            part = part + rs_recv2[n, d].astype(F32)
        out[:, pl.ds(n * cols, cols)] = part.astype(BF16)

    for cp in y_copies + [first] + forwards + m_copies + d_copies + q1 + q2:
        cp.wait_send()
    if span > 1:
        for cp in sq_copies:
            cp.wait_send()

    @pl.when(has_next)
    def _():
        for tt in range(T):
            remote(hidden.at[pl.ds(r - PAD, PAD)], xbuf.at[pl.ds(0, PAD)],
                   hs_sem.at[tt], hr_sem, c + 1, tt).wait_send()

    for d in range(1, C):
        cc = (c + d) % C

        def sent_state(cc=cc, d=d):
            remote(st_send.at[cc // stride], st_recv.at[c], ss_sem.at[d], sr_sem.at[d], cc, t).wait_send()

        def sent_start(cc=cc, d=d):
            remote(start_out.at[cc], start_buf.at[mine], bs_sem.at[d], br_sem.at[d], cc, t).wait_send()

        if stride == 1:
            sent_state()
            sent_start()
        else:
            pl.when(cc % stride == 0)(sent_state)
            pl.when(c % stride == 0)(sent_start)


def body(sizes, hidden, in_weight, step_weight, group_weight, conv_inner, inner_bias, conv_group,
         group_bias, step_bias, log_rate, skip_weight, norm_gain, out_weight):
    C, T = sizes
    Y = T // 2
    r, D = hidden.shape
    R = r * T
    M = R + PAD
    inner = out_weight.shape[0]
    m_dev = group_weight.shape[0]
    NS = min(C, STATE // 16)
    NC = 4
    cols = D // NC
    span = T // GROUPS
    vm = pl.BlockSpec(memory_space=pltpu.VMEM)
    hbm = pl.BlockSpec(memory_space=pl.ANY)
    V = pltpu.VMEM
    S = pltpu.SemaphoreType.DMA
    scratch = [
        V((M, D), BF16),
        V((inner // LANES, D, 2, LANES), BF16),
        V((D // LANES, m_dev, GROUPS, LANES), BF16),
        V((inner, D), BF16),
        V((LANES, D), BF16),
        V((8, LANES), F32),
        V((R + M, 2 * D), BF16),
        V((M, 2 * LANES), F32),
        V((R, inner), BF16),
        V((GROUPS, m_dev, M), BF16),
        V((T, m_dev, M), BF16),
        V((M, 2 * STATE), F32),
        V((R, inner), BF16),
        V((NS, STATE // NS, inner), BF16),
        V((C, STATE // NS, inner), BF16),
        V((8, LANES), F32),
        V((C, 8, LANES), F32),
        V((C, STATE // NS, inner), BF16),
        V((NS, STATE // NS, inner), BF16),
        V((R, inner), BF16),
        V((R, inner), F32),
        V((T, r, inner), BF16),
        V((NC, Y * r, cols), BF16),
        V((NC, Y * r, cols), BF16),
        V((NC, Y, r, cols), F32),
        V((NC, Y, r, cols), BF16),
        V((NC, Y, r, cols), BF16),
        V((R, LANES), F32),
        V((span, R, LANES), F32),
        S((inner // LANES,)), S((D // LANES,)), S, S,
        S((Y,)), S((Y,)), S((Y,)), S((Y,)), S((T,)), S,
        S((T,)), S((T,)), S((C,)), S((C,)), S((C,)), S((C,)), S((C,)), S((C,)),
        S((NC,)), S((NC,)), S((NC, Y)), S((NC, Y)), S((span,)), S((span,)),
    ]
    return pl.pallas_call(
        functools.partial(kernel, sizes),
        out_shape=jax.ShapeDtypeStruct((r, D), BF16),
        in_specs=[hbm, hbm, vm, hbm, vm, vm, vm, vm, vm, vm, vm, vm, hbm],
        out_specs=vm,
        scratch_shapes=scratch,
        compiler_params=pltpu.CompilerParams(
            collective_id=0, has_side_effects=True, vmem_limit_bytes=56 * 1024 * 1024
        ),
        cost_estimate=pl.CostEstimate(flops=8 * R * D * inner, bytes_accessed=16 * D * inner // 2, transcendentals=0),
        name="ssd_block",
    )(
        hidden, in_weight, step_weight.T, group_weight, conv_inner, inner_bias[None, :], conv_group,
        group_bias[None, :], step_bias[None, :], log_rate[None, :], skip_weight[None, :],
        norm_gain[None, :], out_weight,
    )


def solution(mesh):
    sizes = (mesh.shape["ctx"], mesh.shape["tp"])
    placed = (
        P(("ctx", "tp"), None),
        P(None, None, "tp"),
        P(None, "tp"),
        P("tp", None, None),
        P(None, "tp"),
        P("tp"),
        P(),
        P(),
        P("tp"),
        P("tp"),
        P("tp"),
        P("tp"),
        P("tp", None),
    )
    return jax.shard_map(
        functools.partial(body, sizes), mesh=mesh, in_specs=placed,
        out_specs=P(("ctx", "tp"), None), check_vma=False,
    )
```
